512 devices in a mesh: branch: 2 (over z_hi), seq: 32 (over y, z_lo), head: 8 (over x, core).
Axes of the slice: x: 4, y: 4, z: 16 (z_hi: 2, z_lo: 8; z = z_hi * 8 + z_lo), core: 2. Of those that a mesh axis runs over, the one named last changes fastest.
Arguments:
- query_proj: bfloat16 [2, 4096, 3072], P('branch', 'seq', 'head'), may hold values from -120 to 120
- key_proj: bfloat16 [2, 4096, 3072], P('branch', 'seq', 'head'), may hold values from -4 to 4
- value_proj: bfloat16 [2, 4096, 3072], P('branch', 'seq', 'head'), may hold values from -6 to 6
- out_weight: bfloat16 [3072, 3072], P('head'), may hold values from -6 to 6
Outputs:
- projected: bfloat16 [2, 4096, 3072], P('branch', 'seq', 'head')
The draws below stay inside these ranges and needn't reach their ends.
All inputs are finite; a program needn't handle non-finite values.
Results may differ from the reference program's by a relative error of at most 0.02.
Values may be sent and summed in bfloat16 or wider, within the bound.
No kernel may reach another device: no remote copies, remote signals or barrier semaphores. Data moves between devices by JAX's collectives and lax.ppermute only.
A program may use at most 64 MiB of HBM per device.

```python
import math
import jax
import jax.numpy as jnp
from jax import lax

D = 3072
H = 24
DH = 128
TOKENS = 4096
HH = 3072


def shared_keys(key):
    return jnp.clip(jax.random.normal(key, (2, TOKENS, H * DH), jnp.float32), -4.0, 4.0)


def draw_key_proj(key, part):
    base_keys = shared_keys(key)
    return base_keys.astype(jnp.bfloat16)


def draw_query_proj(key, part):
    key = jax.random.fold_in(key, 2)
    drawn_q = jnp.clip(jax.random.normal(key, (2, TOKENS, H * DH), jnp.float32), -4.0, 4.0)
    return drawn_q.astype(jnp.bfloat16)


def raised(entries, rng, source, target, shards_of, factor):
    owner, partner = [(jnp.arange(entries.shape[position]) // (entries.shape[position] // shards_of)).reshape([-1 if axis == position else 1 for axis in range(entries.ndim)]) for position in (source, target)]
    chosen = jax.random.permutation(rng, shards_of)[partner]
    strong = (owner == chosen) | (owner == (partner + shards_of // 2) % shards_of)
    return jnp.where(strong, factor * entries, entries)


def block_scale(own_key, dims, cuts, least, largest):
    def one(axis_at, blocks):
        steps = jax.random.uniform(jax.random.fold_in(jax.random.fold_in(own_key, 6), axis_at), (blocks,), jnp.float32, least / len(cuts), largest / len(cuts))
        return jnp.repeat(jnp.exp(steps), dims[axis_at] // blocks).reshape((-1,) + (1,) * (len(dims) - axis_at - 1))

    loudness = one(*cuts[0])
    for cut in cuts[1:]:
        loudness = loudness * one(*cut)
    return loudness


def gaussian(rng, dims, deviation, most, cuts=(), dtype=jnp.bfloat16):
    array = jax.random.normal(rng, dims, jnp.float32) * deviation
    if len(cuts) > 0:
        array = block_scale(rng, dims, cuts, -0.22, 0.18) * array
    return jnp.clip(array, min=-most, max=most).astype(dtype)


def bell_draw_with(own_key, shape, width, limit, pieces, heavy, kind=jnp.bfloat16):
    result = width * jax.random.normal(own_key, shape, jnp.float32)
    if pieces:
        result = result * block_scale(own_key, shape, pieces, -0.22, 0.18)
    return jnp.clip(raised(result, jax.random.fold_in(own_key, 3), *heavy), -limit, limit).astype(kind)


def setup_inputs(seed: int = 0) -> dict:
    seeds = jax.random.split(jax.random.key(seed), 5)
    return {
        "query_proj": draw_query_proj(jax.random.fold_in(seeds[4], 71), 0),
        "key_proj": draw_key_proj(jax.random.fold_in(seeds[4], 71), 0),
        "value_proj": gaussian(seeds[2], (2, TOKENS, HH), 1.0, 6.0, ((0, 2), (1, 32), (2, 8))),
        "out_weight": bell_draw_with(seeds[3], (HH, D), (0.5 * TOKENS ** 0.5 / (H * DH) ** 0.5), 6.0, ((0, 8),), (0, 1, 8, 2.0)),
    }


def attend_branch(query_rows, key_all, value_all):
    tok_count = query_rows.shape[0]
    key_count = key_all.shape[0]
    score_scale = 1.0 / math.sqrt(DH)
    query_heads = query_rows.reshape(tok_count, H, DH).transpose(1, 0, 2)
    key_heads = key_all.reshape(key_count, H, DH).transpose(1, 0, 2)
    value_heads = value_all.reshape(key_count, H, DH).transpose(1, 0, 2)

    def one_head(packed):
        head_query, head_keys, head_values = packed
        scores = jnp.dot(head_query, head_keys.T, preferred_element_type=jnp.float32) * score_scale
        row_peak = lax.optimization_barrier(jnp.max(scores, axis=1, keepdims=True))
        weights = jnp.exp(scores - row_peak)
        row_total = lax.optimization_barrier(jnp.sum(weights, axis=1, keepdims=True))
        mixed = jnp.dot(weights.astype(jnp.bfloat16), head_values, preferred_element_type=jnp.float32)
        return (mixed / row_total).astype(jnp.bfloat16)
    outputs = lax.map(one_head, (query_heads, key_heads, value_heads))
    return outputs.transpose(1, 0, 2).reshape(tok_count, H * DH)

def reference(query_proj, key_proj, value_proj, out_weight):
    source = attend_branch(query_proj[0], key_proj[0], value_proj[0])
    edited = attend_branch(query_proj[1], jnp.concatenate([key_proj[1], key_proj[0]], axis=0), jnp.concatenate([value_proj[1], value_proj[0]], axis=0))
    source_out = jnp.dot(source, out_weight, preferred_element_type=jnp.float32).astype(jnp.bfloat16)
    edited_out = jnp.dot(edited, out_weight, preferred_element_type=jnp.float32).astype(jnp.bfloat16)
    return jnp.stack([source_out, edited_out], axis=0)
```

```python
import math

import jax
import jax.numpy as jnp
from jax import lax
from jax.experimental import pallas as pl
from jax.experimental.pallas import tpu as pltpu
from jax.sharding import Mesh, PartitionSpec as P

DH = 128
BLOCK = 128
SCALE_LOG2 = math.log2(math.e) / math.sqrt(DH)
TAIL = 16
KEY_AXES = ("branch", "z2", "z1")
ROW_AXES = ("y", "z0")
HEAD_AXES = ("x", "core")


def attend_kernel(edit_ref, q_ref, k_ref, v_ref, out_ref, wide_ref, tail_ref):
    head = pl.program_id(0)
    heads = pl.num_programs(0)
    row_blocks = out_ref.shape[0]
    key_count = k_ref.shape[0]

    def attend(count):
        keys = k_ref[:count, :]
        wide_ref[:count, :DH] = v_ref[:count, :]
        wide_ref[:count, DH:] = jnp.ones((count, DH), jnp.bfloat16)
        for block in range(row_blocks):
            queries = q_ref[block * BLOCK : (block + 1) * BLOCK, :]
            scores = lax.dot_general(
                queries, keys, (((1,), (1,)), ((), ())), preferred_element_type=jnp.float32
            )
            peak = jnp.max(scores, axis=1, keepdims=True)
            weights = jnp.exp2((scores - peak) * SCALE_LOG2).astype(jnp.bfloat16)
            both = jnp.dot(weights, wide_ref[:count, :], preferred_element_type=jnp.float32)
            total = both[:, DH:]
            out_ref[block, pl.ds(pl.multiple_of(head * BLOCK, BLOCK), BLOCK), :] = (
                both[:, :DH] / total
            ).astype(jnp.bfloat16)
            level = peak * SCALE_LOG2 + jnp.log2(total)
            tail_ref[block, pl.ds(head, 1), :] = level.T[:1, :]

    @pl.when(edit_ref[0] == 1)
    def _():
        attend(key_count)

    @pl.when(edit_ref[0] != 1)
    def _():
        attend(key_count // 2)

    @pl.when(head == heads - 1)
    def _():
        level = tail_ref[:, :4, :]
        high = level.astype(jnp.bfloat16).astype(jnp.float32)
        middle = (level - high).astype(jnp.bfloat16).astype(jnp.float32)
        low = level - high - middle
        pieces = jnp.concatenate([high, middle, low, jnp.zeros_like(low)], axis=1)
        out_ref[:, heads_rows(out_ref) :, :] = pieces.astype(jnp.bfloat16)


def heads_rows(ref):
    return ref.shape[1] - TAIL


def attend(edit, queries, keys_values):
    rows, feats = queries.shape
    keys = keys_values.shape[0]
    heads = feats // DH
    blocks = rows // BLOCK
    return pl.pallas_call(
        attend_kernel,
        grid=(heads,),
        out_shape=jax.ShapeDtypeStruct((blocks, heads * BLOCK + TAIL, DH), jnp.bfloat16),
        in_specs=[
            pl.BlockSpec(memory_space=pltpu.SMEM),
            pl.BlockSpec((rows, DH), lambda h: (0, h)),
            pl.BlockSpec((keys, DH), lambda h: (0, h)),
            pl.BlockSpec((keys, DH), lambda h: (0, heads + h)),
        ],
        out_specs=pl.BlockSpec((blocks, heads * BLOCK + TAIL, DH), lambda h: (0, 0, 0)),
        scratch_shapes=[
            pltpu.VMEM((keys, 2 * DH), jnp.bfloat16),
            pltpu.VMEM((blocks, 8, BLOCK), jnp.float32),
        ],
        compiler_params=pltpu.CompilerParams(vmem_limit_bytes=32 * 1024 * 1024),
        cost_estimate=pl.CostEstimate(
            flops=4 * rows * keys * feats,
            bytes_accessed=2 * (2 * rows * feats + 2 * keys * feats),
            transcendentals=rows * keys * heads,
        ),
    )(edit, queries, keys_values, keys_values)


def merge_kernel(parts_ref, out_ref):
    count, height, _ = parts_ref.shape
    heads = (height - TAIL) // BLOCK
    tail = parts_ref[:, height - TAIL :, :].astype(jnp.float32)
    level = tail[:, :4, :] + tail[:, 4:8, :] + tail[:, 8:12, :]
    share = jnp.exp2(level - jnp.max(level, axis=0, keepdims=True))
    share = share / jnp.sum(share, axis=0, keepdims=True)
    flat = jnp.concatenate(
        [share.reshape(count * 4, BLOCK), jnp.zeros((BLOCK - count * 4, BLOCK), jnp.float32)], axis=0
    )
    turned = flat.T
    for head in range(heads):
        total = jnp.zeros((BLOCK, DH), jnp.float32)
        for part in range(count):
            column = part * 4 + head
            values = parts_ref[part, head * BLOCK : (head + 1) * BLOCK, :].astype(jnp.float32)
            total = total + values * turned[:, column : column + 1]
        out_ref[:, head * DH : (head + 1) * DH] = total.astype(jnp.bfloat16)


def merge(parts):
    heads = (parts.shape[1] - TAIL) // BLOCK
    return pl.pallas_call(
        merge_kernel,
        out_shape=jax.ShapeDtypeStruct((BLOCK, heads * DH), jnp.bfloat16),
        compiler_params=pltpu.CompilerParams(vmem_limit_bytes=16 * 1024 * 1024),
        cost_estimate=pl.CostEstimate(
            flops=2 * parts.size, bytes_accessed=2 * parts.size, transcendentals=0
        ),
    )(parts)


def project_kernel(attended_ref, weight_ref, out_ref):
    count, _, feats = attended_ref.shape
    total = jnp.zeros(out_ref.shape, jnp.float32)
    for part in range(count):
        total = total + jnp.dot(
            attended_ref[part],
            weight_ref[part * feats : (part + 1) * feats, :],
            preferred_element_type=jnp.float32,
        )
    out_ref[...] = total.astype(jnp.bfloat16)


def project(attended, weight):
    count, rows, feats = attended.shape
    columns = weight.shape[1]
    return pl.pallas_call(
        project_kernel,
        out_shape=jax.ShapeDtypeStruct((rows, columns), jnp.bfloat16),
        compiler_params=pltpu.CompilerParams(vmem_limit_bytes=16 * 1024 * 1024),
        cost_estimate=pl.CostEstimate(
            flops=2 * count * rows * feats * columns,
            bytes_accessed=2 * (attended.size + weight.size),
            transcendentals=0,
        ),
    )(attended, weight)


def body(query_proj, key_proj, value_proj, out_weight):
    own = jnp.concatenate([key_proj[0], value_proj[0]], axis=1)
    keys_values = lax.all_gather(own, KEY_AXES, axis=0, tiled=True)
    queries = lax.all_gather(query_proj[0], ROW_AXES, axis=0, tiled=True)
    weight = lax.all_to_all(out_weight, HEAD_AXES, split_axis=1, concat_axis=0, tiled=True)
    keys_values, queries, weight = lax.optimization_barrier((keys_values, queries, weight))
    edit = lax.axis_index("branch").astype(jnp.int32).reshape(1)
    partial = attend(edit, queries, keys_values)
    parts = lax.all_to_all(partial, ROW_AXES, split_axis=0, concat_axis=0, tiled=True)
    attended = merge(parts)
    gathered = lax.all_gather(attended, HEAD_AXES, axis=0, tiled=False)
    return project(gathered, weight)[None]


def solution(mesh):
    split = Mesh(
        mesh.devices.reshape(2, 4, 2, 2, 2, 4, 2),
        ("branch", "y", "z2", "z1", "z0", "x", "core"),
    )
    rows = ("y", "z2", "z1", "z0")
    placed = P("branch", rows, HEAD_AXES)
    return jax.shard_map(
        body,
        mesh=split,
        in_specs=(placed, placed, placed, P(HEAD_AXES, None)),
        out_specs=placed,
        check_vma=False,
    )
```

```python
import math

import jax
import jax.numpy as jnp
from jax import lax
from jax.experimental import pallas as pl
from jax.experimental.pallas import tpu as pltpu
from jax.sharding import Mesh, PartitionSpec as P

DH = 128
BLOCK = 128
SCALE_LOG2 = math.log2(math.e) / math.sqrt(DH)
TAIL = 16
KEY_AXES = ("branch", "z2", "z1")
ROW_AXES = ("y", "z0")
HEAD_AXES = ("x", "core")


def attend_kernel(place_ref, q_ref, k_ref, v_ref, out_ref, wide_ref, tail_ref):
    head = pl.program_id(0)
    heads = pl.num_programs(0)
    row_blocks = out_ref.shape[0]
    key_count = k_ref.shape[0]

    def attend(count):
        keys = k_ref[:count, :]
        wide_ref[:count, :DH] = v_ref[:count, :]
        wide_ref[:count, DH:] = jnp.ones((count, DH), jnp.bfloat16)
        for block in range(row_blocks):
            target = block // 2 * 2 + (block % 2 ^ place_ref[1])
            queries = q_ref[block * BLOCK : (block + 1) * BLOCK, :]
            scores = lax.dot_general(
                queries, keys, (((1,), (1,)), ((), ())), preferred_element_type=jnp.float32
            )
            peak = jnp.max(scores, axis=1, keepdims=True)
            weights = jnp.exp2((scores - peak) * SCALE_LOG2).astype(jnp.bfloat16)
            both = jnp.dot(weights, wide_ref[:count, :], preferred_element_type=jnp.float32)
            total = both[:, DH:]
            out_ref[target, pl.ds(pl.multiple_of(head * BLOCK, BLOCK), BLOCK), :] = (
                both[:, :DH] / total
            ).astype(jnp.bfloat16)
            level = peak * SCALE_LOG2 + jnp.log2(total)
            tail_ref[target, pl.ds(head, 1), :] = level.T[:1, :]

    @pl.when(place_ref[0] == 1)
    def _():
        attend(key_count)

    @pl.when(place_ref[0] != 1)
    def _():
        attend(key_count // 2)

    @pl.when(head == heads - 1)
    def _():
        level = tail_ref[:, :4, :]
        high = level.astype(jnp.bfloat16).astype(jnp.float32)
        middle = (level - high).astype(jnp.bfloat16).astype(jnp.float32)
        low = level - high - middle
        pieces = jnp.concatenate([high, middle, low, jnp.zeros_like(low)], axis=1)
        out_ref[:, heads_rows(out_ref) :, :] = pieces.astype(jnp.bfloat16)


def heads_rows(ref):
    return ref.shape[1] - TAIL


def attend(place, queries, keys_values):
    rows, feats = queries.shape
    keys = keys_values.shape[0]
    heads = feats // DH
    blocks = rows // BLOCK
    return pl.pallas_call(
        attend_kernel,
        grid=(heads,),
        out_shape=jax.ShapeDtypeStruct((blocks, heads * BLOCK + TAIL, DH), jnp.bfloat16),
        in_specs=[
            pl.BlockSpec(memory_space=pltpu.SMEM),
            pl.BlockSpec((rows, DH), lambda h: (0, h)),
            pl.BlockSpec((keys, DH), lambda h: (0, h)),
            pl.BlockSpec((keys, DH), lambda h: (0, heads + h)),
        ],
        out_specs=pl.BlockSpec((blocks, heads * BLOCK + TAIL, DH), lambda h: (0, 0, 0)),
        scratch_shapes=[
            pltpu.VMEM((keys, 2 * DH), jnp.bfloat16),
            pltpu.VMEM((blocks, 8, BLOCK), jnp.float32),
        ],
        compiler_params=pltpu.CompilerParams(vmem_limit_bytes=60 * 1024 * 1024),
        cost_estimate=pl.CostEstimate(
            flops=4 * rows * keys * feats,
            bytes_accessed=2 * (2 * rows * feats + 2 * keys * feats),
            transcendentals=rows * keys * heads,
        ),
    )(place, queries, keys_values, keys_values)


def merge_kernel(parts_ref, out_ref):
    count, height, _ = parts_ref.shape
    heads = (height - TAIL) // BLOCK
    tail = parts_ref[:, height - TAIL :, :].astype(jnp.float32)
    level = tail[:, :4, :] + tail[:, 4:8, :] + tail[:, 8:12, :]
    share = jnp.exp2(level - jnp.max(level, axis=0, keepdims=True))
    share = share / jnp.sum(share, axis=0, keepdims=True)
    flat = jnp.concatenate(
        [share.reshape(count * 4, BLOCK), jnp.zeros((BLOCK - count * 4, BLOCK), jnp.float32)], axis=0
    )
    turned = flat.T
    for head in range(heads):
        total = jnp.zeros((BLOCK, DH), jnp.float32)
        for part in range(count):
            column = part * 4 + head
            values = parts_ref[part, head * BLOCK : (head + 1) * BLOCK, :].astype(jnp.float32)
            total = total + values * turned[:, column : column + 1]
        out_ref[:, head * DH : (head + 1) * DH] = total.astype(jnp.bfloat16)


def merge(parts):
    heads = (parts.shape[1] - TAIL) // BLOCK
    return pl.pallas_call(
        merge_kernel,
        out_shape=jax.ShapeDtypeStruct((BLOCK, heads * DH), jnp.bfloat16),
        compiler_params=pltpu.CompilerParams(vmem_limit_bytes=16 * 1024 * 1024),
        cost_estimate=pl.CostEstimate(
            flops=2 * parts.size, bytes_accessed=2 * parts.size, transcendentals=0
        ),
    )(parts)


def project_kernel(attended_ref, weight_ref, out_ref):
    count, _, feats = attended_ref.shape
    total = jnp.zeros(out_ref.shape, jnp.float32)
    for part in range(count):
        total = total + jnp.dot(
            attended_ref[part],
            weight_ref[part * feats : (part + 1) * feats, :],
            preferred_element_type=jnp.float32,
        )
    out_ref[...] = total.astype(jnp.bfloat16)


def project(attended, weight):
    count, rows, feats = attended.shape
    columns = weight.shape[1]
    return pl.pallas_call(
        project_kernel,
        out_shape=jax.ShapeDtypeStruct((rows, columns), jnp.bfloat16),
        compiler_params=pltpu.CompilerParams(vmem_limit_bytes=16 * 1024 * 1024),
        cost_estimate=pl.CostEstimate(
            flops=2 * count * rows * feats * columns,
            bytes_accessed=2 * (attended.size + weight.size),
            transcendentals=0,
        ),
    )(attended, weight)


def body(query_proj, key_proj, value_proj, out_weight):
    own = jnp.concatenate([key_proj[0], value_proj[0]], axis=1)
    keys_values = lax.all_gather(own, KEY_AXES, axis=0, tiled=True)
    beside = lax.ppermute(query_proj[0], "z0", [(0, 1), (1, 0)])
    queries = jnp.concatenate([query_proj[0], beside], axis=0)
    queries = lax.all_gather(queries, "y", axis=0, tiled=True)
    weight = lax.all_to_all(out_weight, HEAD_AXES, split_axis=1, concat_axis=0, tiled=True)
    keys_values, queries, weight = lax.optimization_barrier((keys_values, queries, weight))
    place = jnp.stack([lax.axis_index("branch"), lax.axis_index("z0")]).astype(jnp.int32)
    partial = attend(place, queries, keys_values)
    parts = lax.all_to_all(partial, ROW_AXES, split_axis=0, concat_axis=0, tiled=True)
    attended = merge(parts)
    gathered = lax.all_gather(attended, HEAD_AXES, axis=0, tiled=False)
    return project(gathered, weight)[None]


def solution(mesh):
    split = Mesh(
        mesh.devices.reshape(2, 4, 2, 2, 2, 4, 2),
        ("branch", "y", "z2", "z1", "z0", "x", "core"),
    )
    rows = ("y", "z2", "z1", "z0")
    placed = P("branch", rows, HEAD_AXES)
    return jax.shard_map(
        body,
        mesh=split,
        in_specs=(placed, placed, placed, P(HEAD_AXES, None)),
        out_specs=placed,
        check_vma=False,
    )
```

```python
import math

import jax
import jax.numpy as jnp
from jax import lax
from jax.experimental import pallas as pl
from jax.experimental.pallas import tpu as pltpu
from jax.sharding import Mesh, PartitionSpec as P

DH = 128
BLOCK = 128
KEY_SHIFT = 13
SCALE_LOG2 = math.log2(math.e) / math.sqrt(DH) / 2.0**KEY_SHIFT
TAIL = 16
KEY_AXES = ("branch", "z2", "z1")
ROW_AXES = ("y", "z0")
HEAD_AXES = ("x", "core")


def pack_kernel(key_ref, value_ref, out_ref):
    feats = key_ref.shape[1]
    out_ref[:, :feats] = (key_ref[...].astype(jnp.float32) * 2.0**KEY_SHIFT).astype(jnp.bfloat16)
    values = value_ref[...].astype(jnp.float32)
    largest = jnp.max(jnp.abs(values), axis=1, keepdims=True)
    power = jnp.floor(jnp.log2(jnp.maximum(largest, 2.0**-100)))
    power = jnp.broadcast_to(power, (values.shape[0], DH))
    factor = jnp.exp2(14.0 - power)
    for head in range(feats // DH):
        part = values[:, head * DH : (head + 1) * DH]
        out_ref[:, feats + head * DH : feats + (head + 1) * DH] = (part * factor).astype(jnp.bfloat16)
    out_ref[:, 2 * feats :] = power.astype(jnp.bfloat16)


def pack(keys, values):
    rows, feats = keys.shape
    return pl.pallas_call(
        pack_kernel,
        out_shape=jax.ShapeDtypeStruct((rows, 2 * feats + DH), jnp.bfloat16),
        cost_estimate=pl.CostEstimate(
            flops=4 * rows * feats, bytes_accessed=8 * rows * feats, transcendentals=2 * rows * DH
        ),
    )(keys, values)


def attend_kernel(edit_ref, q_ref, k_ref, v_ref, power_ref, out_ref, wide_ref, tail_ref):
    head = pl.program_id(0)
    heads = pl.num_programs(0)
    row_blocks = out_ref.shape[0]
    key_count = k_ref.shape[0]

    def attend(count):
        keys = k_ref[:count, :]
        factor = jnp.exp2(power_ref[:count, :].astype(jnp.float32) - 14.0)
        wide_ref[:count, :DH] = (v_ref[:count, :].astype(jnp.float32) * factor).astype(jnp.bfloat16)
        wide_ref[:count, DH:] = jnp.ones((count, DH), jnp.bfloat16)
        for block in range(row_blocks):
            queries = q_ref[block * BLOCK : (block + 1) * BLOCK, :]
            scores = lax.dot_general(
                queries, keys, (((1,), (1,)), ((), ())), preferred_element_type=jnp.float32
            )
            peak = jnp.max(scores, axis=1, keepdims=True)
            weights = jnp.exp2((scores - peak) * SCALE_LOG2).astype(jnp.bfloat16)
            both = jnp.dot(weights, wide_ref[:count, :], preferred_element_type=jnp.float32)
            total = both[:, DH:]
            out_ref[block, pl.ds(pl.multiple_of(head * BLOCK, BLOCK), BLOCK), :] = (
                both[:, :DH] / total
            ).astype(jnp.bfloat16)
            level = peak * SCALE_LOG2 + jnp.log2(total)
            tail_ref[block, pl.ds(head, 1), :] = level.T[:1, :]

    @pl.when(edit_ref[0] == 1)
    def _():
        attend(key_count)

    @pl.when(edit_ref[0] != 1)
    def _():
        attend(key_count // 2)

    @pl.when(head == heads - 1)
    def _():
        level = tail_ref[:, :4, :]
        high = level.astype(jnp.bfloat16).astype(jnp.float32)
        middle = (level - high).astype(jnp.bfloat16).astype(jnp.float32)
        low = level - high - middle
        pieces = jnp.concatenate([high, middle, low, jnp.zeros_like(low)], axis=1)
        out_ref[:, out_ref.shape[1] - TAIL :, :] = pieces.astype(jnp.bfloat16)


def attend(edit, queries, packed):
    rows, feats = queries.shape
    keys = packed.shape[0]
    heads = feats // DH
    blocks = rows // BLOCK
    return pl.pallas_call(
        attend_kernel,
        grid=(heads,),
        out_shape=jax.ShapeDtypeStruct((blocks, heads * BLOCK + TAIL, DH), jnp.bfloat16),
        in_specs=[
            pl.BlockSpec(memory_space=pltpu.SMEM),
            pl.BlockSpec((rows, DH), lambda h: (0, h)),
            pl.BlockSpec((keys, DH), lambda h: (0, h)),
            pl.BlockSpec((keys, DH), lambda h: (0, heads + h)),
            pl.BlockSpec((keys, DH), lambda h: (0, 2 * heads)),
        ],
        out_specs=pl.BlockSpec((blocks, heads * BLOCK + TAIL, DH), lambda h: (0, 0, 0)),
        scratch_shapes=[
            pltpu.VMEM((keys, 2 * DH), jnp.bfloat16),
            pltpu.VMEM((blocks, 8, BLOCK), jnp.float32),
        ],
        compiler_params=pltpu.CompilerParams(vmem_limit_bytes=32 * 1024 * 1024),
        cost_estimate=pl.CostEstimate(
            flops=4 * rows * keys * feats,
            bytes_accessed=2 * (2 * rows * feats + 2 * keys * feats),
            transcendentals=rows * keys * heads,
        ),
    )(edit, queries, packed, packed, packed)


def merge_kernel(parts_ref, weight_ref, out_ref):
    count, height, _ = parts_ref.shape
    heads = (height - TAIL) // BLOCK
    columns = out_ref.shape[2]
    tail = parts_ref[:, height - TAIL :, :].astype(jnp.float32)
    level = tail[:, :4, :] + tail[:, 4:8, :] + tail[:, 8:12, :]
    share = jnp.exp2(level - jnp.max(level, axis=0, keepdims=True))
    share = share / jnp.sum(share, axis=0, keepdims=True)
    flat = jnp.concatenate(
        [share.reshape(count * 4, BLOCK), jnp.zeros((BLOCK - count * 4, BLOCK), jnp.float32)], axis=0
    )
    turned = flat.T
    merged = []
    for head in range(heads):
        total = jnp.zeros((BLOCK, DH), jnp.float32)
        for part in range(count):
            column = part * 4 + head
            values = parts_ref[part, head * BLOCK : (head + 1) * BLOCK, :].astype(jnp.float32)
            total = total + values * turned[:, column : column + 1]
        merged.append(total.astype(jnp.bfloat16))
    attended = jnp.concatenate(merged, axis=1)
    for target in range(out_ref.shape[0]):
        out_ref[target] = jnp.dot(
            attended,
            weight_ref[:, target * columns : (target + 1) * columns],
            preferred_element_type=jnp.float32,
        ).astype(jnp.bfloat16)


def merge(parts, weight, targets):
    columns = weight.shape[1] // targets
    return pl.pallas_call(
        merge_kernel,
        out_shape=jax.ShapeDtypeStruct((targets, BLOCK, columns), jnp.bfloat16),
        compiler_params=pltpu.CompilerParams(vmem_limit_bytes=16 * 1024 * 1024),
        cost_estimate=pl.CostEstimate(
            flops=2 * BLOCK * weight.size,
            bytes_accessed=2 * (parts.size + weight.size),
            transcendentals=0,
        ),
    )(parts, weight)


def add_kernel(parts_ref, out_ref):
    total = parts_ref[0].astype(jnp.float32)
    for part in range(1, parts_ref.shape[0]):
        total = total + parts_ref[part].astype(jnp.float32)
    out_ref[...] = total.astype(jnp.bfloat16)


def add(parts):
    return pl.pallas_call(
        add_kernel, out_shape=jax.ShapeDtypeStruct(parts.shape[1:], jnp.bfloat16)
    )(parts)


def spread(value, axes):
    count = lax.axis_size(axes)
    copies = jnp.broadcast_to(value[None], (count,) + value.shape)
    return lax.all_to_all(copies, axes, split_axis=0, concat_axis=0, tiled=True)


def body(query_proj, key_proj, value_proj, out_weight):
    queries = spread(query_proj[0], ROW_AXES).reshape(-1, query_proj.shape[2])
    packed = pack(key_proj[0], value_proj[0]).astype(jnp.float16)
    packed = lax.all_gather(packed, KEY_AXES, axis=0, tiled=True).astype(jnp.bfloat16)
    edit = lax.axis_index("branch").astype(jnp.int32).reshape(1)
    partial = attend(edit, queries, packed)
    parts = lax.all_to_all(partial, ROW_AXES, split_axis=0, concat_axis=0, tiled=True)
    shares = merge(parts, out_weight, lax.axis_size(HEAD_AXES))
    shares = lax.all_to_all(shares, HEAD_AXES, split_axis=0, concat_axis=0, tiled=True)
    return add(shares)[None]


def solution(mesh):
    split = Mesh(
        mesh.devices.reshape(2, 4, 2, 2, 2, 4, 2),
        ("branch", "y", "z2", "z1", "z0", "x", "core"),
    )
    rows = ("y", "z2", "z1", "z0")
    placed = P("branch", rows, HEAD_AXES)
    return jax.shard_map(
        body,
        mesh=split,
        in_specs=(placed, placed, placed, P(HEAD_AXES, None)),
        out_specs=placed,
        check_vma=False,
    )
```

```python
import math

import jax
import jax.numpy as jnp
from jax import lax
from jax.experimental import pallas as pl
from jax.experimental.pallas import tpu as pltpu
from jax.sharding import Mesh, PartitionSpec as P

DH = 128
BLOCK = 128
KEY_SHIFT = 13
SCALE_LOG2 = math.log2(math.e) / math.sqrt(DH) / 2.0**KEY_SHIFT
TAIL = 16
KEY_AXES = ("branch", "z2", "z1")
ROW_AXES = ("y", "z0")
HEAD_AXES = ("x", "core")


def pack_kernel(query_ref, key_ref, value_ref, out_ref, copies_ref):
    for copy in range(copies_ref.shape[0]):
        copies_ref[copy] = query_ref[...]
    feats = key_ref.shape[1]
    out_ref[:, :feats] = (key_ref[...].astype(jnp.float32) * 2.0**KEY_SHIFT).astype(jnp.bfloat16)
    values = value_ref[...].astype(jnp.float32)
    largest = jnp.max(jnp.abs(values), axis=1, keepdims=True)
    power = jnp.floor(jnp.log2(jnp.maximum(largest, 2.0**-100)))
    power = jnp.broadcast_to(power, (values.shape[0], DH))
    factor = jnp.exp2(14.0 - power)
    for head in range(feats // DH):
        part = values[:, head * DH : (head + 1) * DH]
        out_ref[:, feats + head * DH : feats + (head + 1) * DH] = (part * factor).astype(jnp.bfloat16)
    out_ref[:, 2 * feats :] = power.astype(jnp.bfloat16)


def pack(queries, keys, values, copies):
    rows, feats = keys.shape
    return pl.pallas_call(
        pack_kernel,
        out_shape=(
            jax.ShapeDtypeStruct((rows, 2 * feats + DH), jnp.bfloat16),
            jax.ShapeDtypeStruct((copies, rows, feats), jnp.bfloat16),
        ),
        cost_estimate=pl.CostEstimate(
            flops=4 * rows * feats, bytes_accessed=24 * rows * feats, transcendentals=2 * rows * DH
        ),
    )(queries, keys, values)


def attend_kernel(q_ref, k_ref, v_ref, power_ref, out_ref, wide_ref, tail_ref):
    head = pl.program_id(0)
    heads = pl.num_programs(0)
    row_blocks = out_ref.shape[0]
    key_count = k_ref.shape[0]
    edit = lax.axis_index("branch")

    def attend(count):
        keys = k_ref[:count, :]
        factor = jnp.exp2(power_ref[:count, :].astype(jnp.float32) - 14.0)
        wide_ref[:count, :DH] = (v_ref[:count, :].astype(jnp.float32) * factor).astype(jnp.bfloat16)
        wide_ref[:count, DH:] = jnp.ones((count, DH), jnp.bfloat16)
        for block in range(row_blocks):
            queries = q_ref[block * BLOCK : (block + 1) * BLOCK, :]
            scores = lax.dot_general(
                queries, keys, (((1,), (1,)), ((), ())), preferred_element_type=jnp.float32
            )
            peak = jnp.max(scores, axis=1, keepdims=True)
            weights = jnp.exp2((scores - peak) * SCALE_LOG2).astype(jnp.bfloat16)
            both = jnp.dot(weights, wide_ref[:count, :], preferred_element_type=jnp.float32)
            total = both[:, DH:]
            out_ref[block, pl.ds(pl.multiple_of(head * BLOCK, BLOCK), BLOCK), :] = (
                both[:, :DH] / total
            ).astype(jnp.bfloat16)
            level = peak * SCALE_LOG2 + jnp.log2(total)
            tail_ref[block, pl.ds(head, 1), :] = level.T[:1, :]

    @pl.when(edit == 1)
    def _():
        attend(key_count)

    @pl.when(edit != 1)
    def _():
        attend(key_count // 2)

    @pl.when(head == heads - 1)
    def _():
        level = tail_ref[:, :4, :]
        high = level.astype(jnp.bfloat16).astype(jnp.float32)
        middle = (level - high).astype(jnp.bfloat16).astype(jnp.float32)
        low = level - high - middle
        pieces = jnp.concatenate([high, middle, low, jnp.zeros_like(low)], axis=1)
        out_ref[:, out_ref.shape[1] - TAIL :, :] = pieces.astype(jnp.bfloat16)


def attend(queries, packed):
    rows, feats = queries.shape
    keys = packed.shape[0]
    heads = feats // DH
    blocks = rows // BLOCK
    return pl.pallas_call(
        attend_kernel,
        grid=(heads,),
        out_shape=jax.ShapeDtypeStruct((blocks, heads * BLOCK + TAIL, DH), jnp.bfloat16),
        in_specs=[
            pl.BlockSpec((rows, DH), lambda h: (0, h)),
            pl.BlockSpec((keys, DH), lambda h: (0, h)),
            pl.BlockSpec((keys, DH), lambda h: (0, heads + h)),
            pl.BlockSpec((keys, DH), lambda h: (0, 2 * heads)),
        ],
        out_specs=pl.BlockSpec((blocks, heads * BLOCK + TAIL, DH), lambda h: (0, 0, 0)),
        scratch_shapes=[
            pltpu.VMEM((keys, 2 * DH), jnp.bfloat16),
            pltpu.VMEM((blocks, 8, BLOCK), jnp.float32),
        ],
        compiler_params=pltpu.CompilerParams(vmem_limit_bytes=32 * 1024 * 1024),
        cost_estimate=pl.CostEstimate(
            flops=4 * rows * keys * feats,
            bytes_accessed=2 * (2 * rows * feats + 2 * keys * feats),
            transcendentals=rows * keys * heads,
        ),
    )(queries, packed, packed, packed)


def merge_kernel(parts_ref, weight_ref, own_ref, other_ref):
    count, height, _ = parts_ref.shape
    heads = (height - TAIL) // BLOCK
    targets, _, columns = own_ref.shape
    tail = parts_ref[:, height - TAIL :, :].astype(jnp.float32)
    level = tail[:, :4, :] + tail[:, 4:8, :] + tail[:, 8:12, :]
    share = jnp.exp2(level - jnp.max(level, axis=0, keepdims=True))
    share = share / jnp.sum(share, axis=0, keepdims=True)
    flat = jnp.concatenate(
        [share.reshape(count * 4, BLOCK), jnp.zeros((BLOCK - count * 4, BLOCK), jnp.float32)], axis=0
    )
    turned = flat.T
    merged = []
    for head in range(heads):
        total = jnp.zeros((BLOCK, DH), jnp.float32)
        for part in range(count):
            column = part * 4 + head
            values = parts_ref[part, head * BLOCK : (head + 1) * BLOCK, :].astype(jnp.float32)
            total = total + values * turned[:, column : column + 1]
        merged.append(total.astype(jnp.bfloat16))
    attended = jnp.concatenate(merged, axis=1)

    def project(block):
        return jnp.dot(
            attended,
            weight_ref[:, block * columns : (block + 1) * columns],
            preferred_element_type=jnp.float32,
        ).astype(jnp.bfloat16)

    for core in range(2):

        @pl.when(lax.axis_index("core") == core)
        def _():
            for target in range(targets):
                own_ref[target] = project(2 * target + core)
                other_ref[target] = project(2 * target + 1 - core)


def merge(parts, weight, targets):
    columns = weight.shape[1] // (2 * targets)
    half = jax.ShapeDtypeStruct((targets, BLOCK, columns), jnp.bfloat16)
    return pl.pallas_call(
        merge_kernel,
        out_shape=(half, half),
        compiler_params=pltpu.CompilerParams(vmem_limit_bytes=16 * 1024 * 1024),
        cost_estimate=pl.CostEstimate(
            flops=2 * BLOCK * weight.size,
            bytes_accessed=2 * (parts.size + weight.size),
            transcendentals=0,
        ),
    )(parts, weight)


def body(query_proj, key_proj, value_proj, out_weight):
    packed, copies = pack(query_proj[0], key_proj[0], value_proj[0], lax.axis_size(ROW_AXES))
    queries = lax.all_to_all(copies, ROW_AXES, split_axis=0, concat_axis=0, tiled=True)
    queries = queries.reshape(-1, queries.shape[2])
    packed = packed.astype(jnp.float16)
    packed = lax.all_gather(packed, KEY_AXES, axis=0, tiled=True).astype(jnp.bfloat16)
    partial = attend(queries, packed)
    parts = lax.all_to_all(partial, ROW_AXES, split_axis=0, concat_axis=0, tiled=True)
    own, other = merge(parts, out_weight, lax.axis_size("x"))
    other = lax.ppermute(other, "core", [(0, 1), (1, 0)])
    shares = (own.astype(jnp.float32) + other.astype(jnp.float32)).astype(jnp.bfloat16)
    shares = lax.all_to_all(shares, "x", split_axis=0, concat_axis=0, tiled=True)
    return shares.astype(jnp.float32).sum(axis=0).astype(jnp.bfloat16)[None]


def solution(mesh):
    split = Mesh(
        mesh.devices.reshape(2, 4, 2, 2, 2, 4, 2),
        ("branch", "y", "z2", "z1", "z0", "x", "core"),
    )
    rows = ("y", "z2", "z1", "z0")
    placed = P("branch", rows, HEAD_AXES)
    return jax.shard_map(
        body,
        mesh=split,
        in_specs=(placed, placed, placed, P(HEAD_AXES, None)),
        out_specs=placed,
        check_vma=False,
    )
```

```python
import math

import jax
import jax.numpy as jnp
from jax import lax
from jax.experimental import pallas as pl
from jax.experimental.pallas import tpu as pltpu
from jax.sharding import Mesh, PartitionSpec as P

DH = 128
BLOCK = 128
SCALE_LOG2 = math.log2(math.e) / math.sqrt(DH)
TAIL = 16
KEY_AXES = ("branch", "z2", "z1")
ROW_AXES = ("y", "z0")
HEAD_AXES = ("x", "core")


def attend_kernel(q_ref, own_ref, *refs):
    up_refs, down_refs = refs[:4], refs[4:7]
    out_ref, keys_ref, wide_ref, tail_ref = refs[7:]
    row_blocks = out_ref.shape[0]
    feats = q_ref.shape[1]
    heads = feats // DH

    def place(block_ref, slot):
        rows = pl.ds(pl.multiple_of(slot * BLOCK, BLOCK), BLOCK)
        keys_ref[rows, :] = block_ref[:, :feats]
        for head in range(heads):
            wide_ref[head, rows, :DH] = block_ref[:, feats + head * DH : feats + (head + 1) * DH]

    def attend(count):
        for head in range(heads):
            wide_ref[head, :count, DH:] = jnp.ones((count, DH), jnp.bfloat16)
            lanes = slice(head * DH, (head + 1) * DH)
            for block in range(row_blocks):
                queries = q_ref[block * BLOCK : (block + 1) * BLOCK, lanes]
                scores = lax.dot_general(
                    queries,
                    keys_ref[:count, lanes],
                    (((1,), (1,)), ((), ())),
                    preferred_element_type=jnp.float32,
                )
                peak = jnp.max(scores, axis=1, keepdims=True)
                weights = jnp.exp2((scores - peak) * SCALE_LOG2).astype(jnp.bfloat16)
                both = jnp.dot(
                    weights, wide_ref[head, :count, :], preferred_element_type=jnp.float32
                )
                total = both[:, DH:]
                out_ref[block, head * BLOCK : (head + 1) * BLOCK, :] = (
                    both[:, :DH] / total
                ).astype(jnp.bfloat16)
                level = peak * SCALE_LOG2 + jnp.log2(total)
                tail_ref[block, head : head + 1, :] = level.T[:1, :]

    edit = lax.axis_index("branch")
    index = 2 * lax.axis_index("z2") + lax.axis_index("z1")

    @pl.when(edit == 1)
    def _():
        for slot, block_ref in enumerate((own_ref,) + tuple(up_refs) + tuple(down_refs)):
            place(block_ref, slot)
        attend(8 * BLOCK)

    @pl.when(edit != 1)
    def _():
        place(own_ref, index)
        for step in range(1, 4):

            @pl.when(index - step >= 0)
            def _():
                place(up_refs[step - 1], index - step)

            @pl.when(index + step < 4)
            def _():
                place(down_refs[step - 1], index + step)

        attend(4 * BLOCK)

    level = tail_ref[:, :4, :]
    high = level.astype(jnp.bfloat16).astype(jnp.float32)
    middle = (level - high).astype(jnp.bfloat16).astype(jnp.float32)
    low = level - high - middle
    pieces = jnp.concatenate([high, middle, low, jnp.zeros_like(low)], axis=1)
    out_ref[:, heads * BLOCK :, :] = pieces.astype(jnp.bfloat16)


def attend(queries, own, up, down):
    rows, feats = queries.shape
    keys = 8 * BLOCK
    heads = feats // DH
    blocks = rows // BLOCK
    return pl.pallas_call(
        attend_kernel,
        out_shape=jax.ShapeDtypeStruct((blocks, heads * BLOCK + TAIL, DH), jnp.bfloat16),
        scratch_shapes=[
            pltpu.VMEM((keys, feats), jnp.bfloat16),
            pltpu.VMEM((heads, keys, 2 * DH), jnp.bfloat16),
            pltpu.VMEM((blocks, 8, BLOCK), jnp.float32),
        ],
        compiler_params=pltpu.CompilerParams(vmem_limit_bytes=32 * 1024 * 1024),
        cost_estimate=pl.CostEstimate(
            flops=4 * rows * keys * feats,
            bytes_accessed=2 * (2 * rows * feats + 2 * keys * feats),
            transcendentals=rows * keys * heads,
        ),
    )(queries, own, *up, *down)


def merge_kernel(parts_ref, weight_ref, own_ref, other_ref):
    count, height, _ = parts_ref.shape
    heads = (height - TAIL) // BLOCK
    targets, _, columns = own_ref.shape
    tail = parts_ref[:, height - TAIL :, :].astype(jnp.float32)
    level = tail[:, :4, :] + tail[:, 4:8, :] + tail[:, 8:12, :]
    share = jnp.exp2(level - jnp.max(level, axis=0, keepdims=True))
    share = share / jnp.sum(share, axis=0, keepdims=True)
    flat = jnp.concatenate(
        [share.reshape(count * 4, BLOCK), jnp.zeros((BLOCK - count * 4, BLOCK), jnp.float32)], axis=0
    )
    turned = flat.T
    merged = []
    for head in range(heads):
        total = jnp.zeros((BLOCK, DH), jnp.float32)
        for part in range(count):
            column = part * 4 + head
            values = parts_ref[part, head * BLOCK : (head + 1) * BLOCK, :].astype(jnp.float32)
            total = total + values * turned[:, column : column + 1]
        merged.append(total.astype(jnp.bfloat16))
    attended = jnp.concatenate(merged, axis=1)

    def project(block):
        return jnp.dot(
            attended,
            weight_ref[:, block * columns : (block + 1) * columns],
            preferred_element_type=jnp.float32,
        ).astype(jnp.bfloat16)

    for core in range(2):

        @pl.when(lax.axis_index("core") == core)
        def _():
            for target in range(targets):
                own_ref[target] = project(2 * target + core)
                other_ref[target] = project(2 * target + 1 - core)


def merge(parts, weight, targets):
    columns = weight.shape[1] // (2 * targets)
    half = jax.ShapeDtypeStruct((targets, BLOCK, columns), jnp.bfloat16)
    return pl.pallas_call(
        merge_kernel,
        out_shape=(half, half),
        compiler_params=pltpu.CompilerParams(vmem_limit_bytes=16 * 1024 * 1024),
        cost_estimate=pl.CostEstimate(
            flops=2 * BLOCK * weight.size,
            bytes_accessed=2 * (parts.size + weight.size),
            transcendentals=0,
        ),
    )(parts, weight)


def spread(value, axes):
    count = lax.axis_size(axes)
    copies = jnp.broadcast_to(value[None], (count,) + value.shape)
    return lax.all_to_all(copies, axes, split_axis=0, concat_axis=0, tiled=True)


def ring_pairs(step, turn):
    pairs = []
    for sender in range(8):
        block = (sender - turn * (step - 1)) % 8
        target = (sender + turn) % 8
        if block < 4 or (sender >= 4 and target >= 4):
            pairs.append((sender, target))
    return pairs


def body(query_proj, key_proj, value_proj, out_weight):
    own = jnp.concatenate([key_proj[0], value_proj[0]], axis=1)
    query = query_proj[0]
    beside = lax.ppermute(query, "z0", [(0, 1), (1, 0)])
    up, down = [own], [own]
    for step in range(1, 5):
        up.append(lax.ppermute(up[-1], KEY_AXES, ring_pairs(step, 1)))
        if step < 4:
            down.append(lax.ppermute(down[-1], KEY_AXES, ring_pairs(step, -1)))
        if step == 1:
            beside, up[1] = lax.optimization_barrier((beside, up[1]))
            first = lax.axis_index("z0") == 0
            pair = jnp.concatenate(
                [jnp.where(first, query, beside), jnp.where(first, beside, query)], axis=0
            )
            queries = spread(pair, "y").reshape(-1, query.shape[1])
    partial = attend(queries, own, up[1:], down[1:])
    parts = lax.all_to_all(partial, ROW_AXES, split_axis=0, concat_axis=0, tiled=True)
    own, other = merge(parts, out_weight, lax.axis_size("x"))
    other = lax.ppermute(other, "core", [(0, 1), (1, 0)])
    shares = (own.astype(jnp.float32) + other.astype(jnp.float32)).astype(jnp.bfloat16)
    shares = lax.all_to_all(shares, "x", split_axis=0, concat_axis=0, tiled=True)
    return shares.astype(jnp.float32).sum(axis=0).astype(jnp.bfloat16)[None]


def solution(mesh):
    split = Mesh(
        mesh.devices.reshape(2, 4, 2, 2, 2, 4, 2),
        ("branch", "y", "z2", "z1", "z0", "x", "core"),
    )
    rows = ("y", "z2", "z1", "z0")
    placed = P("branch", rows, HEAD_AXES)
    return jax.shard_map(
        body,
        mesh=split,
        in_specs=(placed, placed, placed, P(HEAD_AXES, None)),
        out_specs=placed,
        check_vma=False,
    )
```

```python
import math

import jax
import jax.numpy as jnp
from jax import lax
from jax.experimental import pallas as pl
from jax.experimental.pallas import tpu as pltpu
from jax.sharding import Mesh, PartitionSpec as P

DH = 128
BLOCK = 128
SCALE_LOG2 = math.log2(math.e) / math.sqrt(DH)
TAIL = 16
KEY_AXES = ("branch", "z2", "z1")
ROW_AXES = ("y", "z0")
HEAD_AXES = ("x", "core")


def attend_kernel(q_ref, own_ref, *refs):
    up_refs, down_refs = refs[:4], refs[4:7]
    out_ref, keys_ref, wide_ref, tail_ref = refs[7:]
    row_blocks = out_ref.shape[0]
    feats = q_ref.shape[1]
    heads = feats // DH

    def place(block_ref, slot):
        rows = pl.ds(pl.multiple_of(slot * BLOCK, BLOCK), BLOCK)
        keys_ref[rows, :] = block_ref[:, :feats]
        for head in range(heads):
            wide_ref[head, rows, :DH] = block_ref[:, feats + head * DH : feats + (head + 1) * DH]

    def attend(count):
        for head in range(heads):
            wide_ref[head, :count, DH:] = jnp.ones((count, DH), jnp.bfloat16)
            lanes = slice(head * DH, (head + 1) * DH)
            for block in range(row_blocks):
                target = block // 2 * 2 + (block % 2 ^ side)
                queries = q_ref[block * BLOCK : (block + 1) * BLOCK, lanes]
                scores = lax.dot_general(
                    queries,
                    keys_ref[:count, lanes],
                    (((1,), (1,)), ((), ())),
                    preferred_element_type=jnp.float32,
                )
                peak = jnp.max(scores, axis=1, keepdims=True)
                weights = jnp.exp2((scores - peak) * SCALE_LOG2).astype(jnp.bfloat16)
                both = jnp.dot(
                    weights, wide_ref[head, :count, :], preferred_element_type=jnp.float32
                )
                total = both[:, DH:]
                out_ref[target, head * BLOCK : (head + 1) * BLOCK, :] = (
                    both[:, :DH] / total
                ).astype(jnp.bfloat16)
                level = peak * SCALE_LOG2 + jnp.log2(total)
                tail_ref[target, head : head + 1, :] = level.T[:1, :]

    side = lax.axis_index("z0")
    edit = lax.axis_index("branch")
    index = 2 * lax.axis_index("z2") + lax.axis_index("z1")

    @pl.when(edit == 1)
    def _():
        for slot, block_ref in enumerate((own_ref,) + tuple(up_refs) + tuple(down_refs)):
            place(block_ref, slot)
        attend(8 * BLOCK)

    @pl.when(edit != 1)
    def _():
        place(own_ref, index)
        for step in range(1, 4):

            @pl.when(index - step >= 0)
            def _():
                place(up_refs[step - 1], index - step)

            @pl.when(index + step < 4)
            def _():
                place(down_refs[step - 1], index + step)

        attend(4 * BLOCK)

    level = tail_ref[:, :4, :]
    high = level.astype(jnp.bfloat16).astype(jnp.float32)
    middle = (level - high).astype(jnp.bfloat16).astype(jnp.float32)
    low = level - high - middle
    pieces = jnp.concatenate([high, middle, low, jnp.zeros_like(low)], axis=1)
    out_ref[:, heads * BLOCK :, :] = pieces.astype(jnp.bfloat16)


def attend(queries, own, up, down):
    rows, feats = queries.shape
    keys = 8 * BLOCK
    heads = feats // DH
    blocks = rows // BLOCK
    return pl.pallas_call(
        attend_kernel,
        out_shape=jax.ShapeDtypeStruct((blocks, heads * BLOCK + TAIL, DH), jnp.bfloat16),
        scratch_shapes=[
            pltpu.VMEM((keys, feats), jnp.bfloat16),
            pltpu.VMEM((heads, keys, 2 * DH), jnp.bfloat16),
            pltpu.VMEM((blocks, 8, BLOCK), jnp.float32),
        ],
        compiler_params=pltpu.CompilerParams(vmem_limit_bytes=32 * 1024 * 1024),
        cost_estimate=pl.CostEstimate(flops=0, bytes_accessed=0, transcendentals=0),
    )(queries, own, *up, *down)


def merge_kernel(parts_ref, weight_ref, own_ref, other_ref):
    count, height, _ = parts_ref.shape
    heads = (height - TAIL) // BLOCK
    targets, _, columns = own_ref.shape
    tail = parts_ref[:, height - TAIL :, :].astype(jnp.float32)
    level = tail[:, :4, :] + tail[:, 4:8, :] + tail[:, 8:12, :]
    share = jnp.exp2(level - jnp.max(level, axis=0, keepdims=True))
    share = share / jnp.sum(share, axis=0, keepdims=True)
    flat = jnp.concatenate(
        [share.reshape(count * 4, BLOCK), jnp.zeros((BLOCK - count * 4, BLOCK), jnp.float32)], axis=0
    )
    turned = flat.T
    merged = []
    for head in range(heads):
        total = jnp.zeros((BLOCK, DH), jnp.float32)
        for part in range(count):
            column = part * 4 + head
            values = parts_ref[part, head * BLOCK : (head + 1) * BLOCK, :].astype(jnp.float32)
            total = total + values * turned[:, column : column + 1]
        merged.append(total.astype(jnp.bfloat16))
    attended = jnp.concatenate(merged, axis=1)

    def project(block):
        return jnp.dot(
            attended,
            weight_ref[:, block * columns : (block + 1) * columns],
            preferred_element_type=jnp.float32,
        ).astype(jnp.bfloat16)

    for core in range(2):

        @pl.when(lax.axis_index("core") == core)
        def _():
            for target in range(targets):
                own_ref[target] = project(2 * target + core)
                other_ref[target] = project(2 * target + 1 - core)


def merge(parts, weight, targets):
    columns = weight.shape[1] // (2 * targets)
    half = jax.ShapeDtypeStruct((targets, BLOCK, columns), jnp.bfloat16)
    return pl.pallas_call(
        merge_kernel,
        out_shape=(half, half),
        compiler_params=pltpu.CompilerParams(vmem_limit_bytes=16 * 1024 * 1024),
        cost_estimate=pl.CostEstimate(
            flops=2 * BLOCK * weight.size,
            bytes_accessed=2 * (parts.size + weight.size),
            transcendentals=0,
        ),
    )(parts, weight)


def spread(value, axes):
    count = lax.axis_size(axes)
    copies = jnp.broadcast_to(value[None], (count,) + value.shape)
    return lax.all_to_all(copies, axes, split_axis=0, concat_axis=0, tiled=True)


def ring_pairs(step, turn):
    pairs = []
    for sender in range(8):
        block = (sender - turn * (step - 1)) % 8
        target = (sender + turn) % 8
        if block < 4 or (sender >= 4 and target >= 4):
            pairs.append((sender, target))
    return pairs


def body(query_proj, key_proj, value_proj, out_weight):
    own = jnp.concatenate([key_proj[0], value_proj[0]], axis=1)
    query = query_proj[0]
    beside = lax.ppermute(query, "z0", [(0, 1), (1, 0)])
    up, down = [own], [own]
    for step in range(1, 5):
        up.append(lax.ppermute(up[-1], KEY_AXES, ring_pairs(step, 1)))
        if step < 4:
            down.append(lax.ppermute(down[-1], KEY_AXES, ring_pairs(step, -1)))
        if step == 1:
            beside, up[1] = lax.optimization_barrier((beside, up[1]))
            pair = jnp.concatenate([query, beside], axis=0)
            queries = spread(pair, "y").reshape(-1, query.shape[1])
    partial = attend(queries, own, up[1:], down[1:])
    parts = lax.all_to_all(partial, ROW_AXES, split_axis=0, concat_axis=0, tiled=True)
    own, other = merge(parts, out_weight, lax.axis_size("x"))
    other = lax.ppermute(other, "core", [(0, 1), (1, 0)])
    shares = (own.astype(jnp.float32) + other.astype(jnp.float32)).astype(jnp.bfloat16)
    shares = lax.all_to_all(shares, "x", split_axis=0, concat_axis=0, tiled=True)
    return shares.astype(jnp.float32).sum(axis=0).astype(jnp.bfloat16)[None]


def solution(mesh):
    split = Mesh(
        mesh.devices.reshape(2, 4, 2, 2, 2, 4, 2),
        ("branch", "y", "z2", "z1", "z0", "x", "core"),
    )
    rows = ("y", "z2", "z1", "z0")
    placed = P("branch", rows, HEAD_AXES)
    return jax.shard_map(
        body,
        mesh=split,
        in_specs=(placed, placed, placed, P(HEAD_AXES, None)),
        out_specs=placed,
        check_vma=False,
    )
```

```python
import math

import jax
import jax.numpy as jnp
from jax import lax
from jax.experimental import pallas as pl
from jax.experimental.pallas import tpu as pltpu
from jax.sharding import Mesh, PartitionSpec as P

DH = 128
BLOCK = 128
SCALE_LOG2 = math.log2(math.e) / math.sqrt(DH)
TAIL = 16
KEY_AXES = ("branch", "z2", "z1")
ROW_AXES = ("y", "z0")
HEAD_AXES = ("x", "core")


def attend_kernel(q_ref, own_ref, *refs):
    up_refs, down_refs = refs[:4], refs[4:7]
    out_ref, keys_ref, wide_ref, tail_ref = refs[7:]
    row_blocks = out_ref.shape[0]
    feats = q_ref.shape[1]
    heads = feats // DH

    def place(block_ref, slot):
        rows = pl.ds(pl.multiple_of(slot * BLOCK, BLOCK), BLOCK)
        keys_ref[rows, :] = block_ref[:, :feats]
        for head in range(heads):
            wide_ref[head, rows, :DH] = block_ref[:, feats + head * DH : feats + (head + 1) * DH]

    def attend(count):
        for head in range(heads):
            wide_ref[head, :count, DH:] = jnp.ones((count, DH), jnp.bfloat16)
            lanes = slice(head * DH, (head + 1) * DH)
            for block in range(row_blocks):
                target = block // 2 * 2 + (block % 2 ^ side)
                queries = q_ref[block * BLOCK : (block + 1) * BLOCK, lanes]
                scores = lax.dot_general(
                    queries,
                    keys_ref[:count, lanes],
                    (((1,), (1,)), ((), ())),
                    preferred_element_type=jnp.float32,
                )
                peak = jnp.max(scores, axis=1, keepdims=True)
                weights = jnp.exp2((scores - peak) * SCALE_LOG2).astype(jnp.bfloat16)
                both = jnp.dot(
                    weights, wide_ref[head, :count, :], preferred_element_type=jnp.float32
                )
                total = both[:, DH:]
                out_ref[target, head * BLOCK : (head + 1) * BLOCK, :] = (
                    both[:, :DH] / total
                ).astype(jnp.bfloat16)
                level = peak * SCALE_LOG2 + jnp.log2(total)
                tail_ref[target, head : head + 1, :] = level.T[:1, :]

    side = lax.axis_index("z0")
    edit = lax.axis_index("branch")
    index = 2 * lax.axis_index("z2") + lax.axis_index("z1")

    @pl.when(edit == 1)
    def _():
        for slot, block_ref in enumerate((own_ref,) + tuple(up_refs) + tuple(down_refs)):
            place(block_ref, slot)
        attend(8 * BLOCK)

    @pl.when(edit != 1)
    def _():
        place(own_ref, index)
        for step in range(1, 4):

            @pl.when(index - step >= 0)
            def _():
                place(up_refs[step - 1], index - step)

            @pl.when(index + step < 4)
            def _():
                place(down_refs[step - 1], index + step)

        attend(4 * BLOCK)

    level = tail_ref[:, :4, :]
    high = level.astype(jnp.bfloat16).astype(jnp.float32)
    middle = (level - high).astype(jnp.bfloat16).astype(jnp.float32)
    low = level - high - middle
    pieces = jnp.concatenate([high, middle, low, jnp.zeros_like(low)], axis=1)
    out_ref[:, heads * BLOCK :, :] = pieces.astype(jnp.bfloat16)


def attend(queries, own, up, down):
    rows, feats = queries.shape
    keys = 8 * BLOCK
    heads = feats // DH
    blocks = rows // BLOCK
    return pl.pallas_call(
        attend_kernel,
        out_shape=jax.ShapeDtypeStruct((blocks, heads * BLOCK + TAIL, DH), jnp.bfloat16),
        scratch_shapes=[
            pltpu.VMEM((keys, feats), jnp.bfloat16),
            pltpu.VMEM((heads, keys, 2 * DH), jnp.bfloat16),
            pltpu.VMEM((blocks, 8, BLOCK), jnp.float32),
        ],
        compiler_params=pltpu.CompilerParams(vmem_limit_bytes=32 * 1024 * 1024),
        cost_estimate=pl.CostEstimate(
            flops=4 * rows * keys * feats,
            bytes_accessed=2 * (2 * rows * feats + 2 * keys * feats),
            transcendentals=rows * keys * heads,
        ),
    )(queries, own, *up, *down)


def merge_kernel(parts_ref, weight_ref, own_ref, other_ref):
    count, height, _ = parts_ref.shape
    heads = (height - TAIL) // BLOCK
    targets, _, columns = own_ref.shape
    tail = parts_ref[:, height - TAIL :, :].astype(jnp.float32)
    level = tail[:, :4, :] + tail[:, 4:8, :] + tail[:, 8:12, :]
    share = jnp.exp2(level - jnp.max(level, axis=0, keepdims=True))
    share = share / jnp.sum(share, axis=0, keepdims=True)
    flat = jnp.concatenate(
        [share.reshape(count * 4, BLOCK), jnp.zeros((BLOCK - count * 4, BLOCK), jnp.float32)], axis=0
    )
    turned = flat.T
    merged = []
    for head in range(heads):
        total = jnp.zeros((BLOCK, DH), jnp.float32)
        for part in range(count):
            column = part * 4 + head
            values = parts_ref[part, head * BLOCK : (head + 1) * BLOCK, :].astype(jnp.float32)
            total = total + values * turned[:, column : column + 1]
        merged.append(total.astype(jnp.bfloat16))
    attended = jnp.concatenate(merged, axis=1)

    def project(block):
        return jnp.dot(
            attended,
            weight_ref[:, block * columns : (block + 1) * columns],
            preferred_element_type=jnp.float32,
        ).astype(jnp.bfloat16)

    for core in range(2):

        @pl.when(lax.axis_index("core") == core)
        def _():
            for target in range(targets):
                own_ref[target] = project(2 * target + core)
                other_ref[target] = project(2 * target + 1 - core)


def merge(parts, weight, targets):
    columns = weight.shape[1] // (2 * targets)
    half = jax.ShapeDtypeStruct((targets, BLOCK, columns), jnp.bfloat16)
    return pl.pallas_call(
        merge_kernel,
        out_shape=(half, half),
        compiler_params=pltpu.CompilerParams(vmem_limit_bytes=16 * 1024 * 1024),
        cost_estimate=pl.CostEstimate(
            flops=2 * BLOCK * weight.size,
            bytes_accessed=2 * (parts.size + weight.size),
            transcendentals=0,
        ),
    )(parts, weight)


def spread(value, axes):
    count = lax.axis_size(axes)
    copies = jnp.broadcast_to(value[None], (count,) + value.shape)
    return lax.all_to_all(copies, axes, split_axis=0, concat_axis=0, tiled=True)


def ring_pairs(step, turn):
    pairs = []
    for sender in range(8):
        block = (sender - turn * (step - 1)) % 8
        target = (sender + turn) % 8
        if block < 4 or (sender >= 4 and target >= 4):
            pairs.append((sender, target))
    return pairs


def body(query_proj, key_proj, value_proj, out_weight):
    own = jnp.concatenate([key_proj[0], value_proj[0]], axis=1)
    query = query_proj[0]
    beside = lax.ppermute(query, "z0", [(0, 1), (1, 0)])
    up, down = [own], [own]
    for step in range(1, 5):
        up.append(lax.ppermute(up[-1], KEY_AXES, ring_pairs(step, 1)))
        if step < 4:
            down.append(lax.ppermute(down[-1], KEY_AXES, ring_pairs(step, -1)))
        if step == 1:
            beside = lax.optimization_barrier((beside, up[1]))[0]
            pair = jnp.concatenate([query, beside], axis=0)
            queries = spread(pair, "y").reshape(-1, query.shape[1])
    partial = attend(queries, own, up[1:], down[1:])
    parts = lax.all_to_all(partial, ROW_AXES, split_axis=0, concat_axis=0, tiled=True)
    own, other = merge(parts, out_weight, lax.axis_size("x"))
    other = lax.ppermute(other, "core", [(0, 1), (1, 0)])
    shares = (own.astype(jnp.float32) + other.astype(jnp.float32)).astype(jnp.bfloat16)
    shares = lax.all_to_all(shares, "x", split_axis=0, concat_axis=0, tiled=True)
    return shares.astype(jnp.float32).sum(axis=0).astype(jnp.bfloat16)[None]


def solution(mesh):
    split = Mesh(
        mesh.devices.reshape(2, 4, 2, 2, 2, 4, 2),
        ("branch", "y", "z2", "z1", "z0", "x", "core"),
    )
    rows = ("y", "z2", "z1", "z0")
    placed = P("branch", rows, HEAD_AXES)
    return jax.shard_map(
        body,
        mesh=split,
        in_specs=(placed, placed, placed, P(HEAD_AXES, None)),
        out_specs=placed,
        check_vma=False,
    )
```
